512 devices in a mesh: row: 4 (over z_lo), col: 16 (over z_hi, x, core), par: 8 (over y).
Axes of the slice: x: 4, y: 8, z: 8 (z_hi: 2, z_lo: 4; z = z_hi * 4 + z_lo), core: 2. Of those that a mesh axis runs over, the one named last changes fastest.
Arguments:
- log_derivs: float32 [8192, 4096], P(('row', 'col'), 'par'), may hold values from -0.09375 to 0.09375
- sample_vector: float32 [8192], P(('row', 'col')), may hold values from -6 to 6
Outputs:
- gram_tiles: float32 [2048, 4, 8192], P(('col', 'par'), None, 'row')
- projected: float32 [4096], P('par')
The draws below stay inside these ranges and needn't reach their ends.
All inputs are finite; a program needn't handle non-finite values.
Results may differ from the reference program's by a relative error of at most 0.0001.
Values sent between devices are 32-bit elements; how exact they have to be, the bound alone decides.
No kernel may reach another device: no remote copies, remote signals or barrier semaphores. Data moves between devices by JAX's collectives and lax.ppermute only.
A program may use at most 64 MiB of HBM per device.

```python
import jax
import jax.numpy as jnp
from jax import lax

P_SIZE = 4096
ROWBLK = 2048
S = 8192
N_ROW = 4


def level_of(stream_key, extent, split, low, largest):
    factor_of = 1.0
    for dim, parts in split:
        steps = jax.random.uniform(jax.random.fold_in(jax.random.fold_in(stream_key, 6), dim), (parts,), jnp.float32, low / len(split), largest / len(split))
        factor_of = factor_of * jnp.repeat(jnp.exp(steps), extent[dim] // parts).reshape((-1,) + (1,) * (len(extent) - 1 - dim))
    return factor_of


def noise(key, shape, scale, reach, cuts=(), held_as=jnp.bfloat16):
    drawn = scale * jax.random.normal(key, shape, jnp.float32)
    if cuts:
        drawn = drawn * level_of(key, shape, cuts, -0.22, 0.18)
    return jnp.clip(drawn, -reach, reach).astype(held_as)


def setup_inputs(seed: int = 0) -> dict:
    key_of = jax.random.split(jax.random.key(seed), 3)
    return {
        "log_derivs": noise(key_of[0], (S, P_SIZE), (P_SIZE ** -0.5), 0.09375, ((0, 64), (1, 8)), jnp.float32),
        "sample_vector": noise(key_of[1], (S,), 1.0, 6.0, ((0, 64),), jnp.float32),
    }


def reference(log_derivs, sample_vector):
    gram = jnp.dot(log_derivs, log_derivs.T, precision=lax.Precision.HIGHEST, preferred_element_type=jnp.float32)
    gram_tiles = gram.reshape(N_ROW, ROWBLK, S).transpose(1, 0, 2)
    projected = jnp.dot(sample_vector, log_derivs, precision=lax.Precision.HIGHEST, preferred_element_type=jnp.float32)
    return gram_tiles, projected
```

```python
import jax
import jax.numpy as jnp
from jax import lax
from jax.experimental import pallas as pl
from jax.experimental.pallas import tpu as pltpu
from jax.sharding import Mesh, PartitionSpec as P

AXES = ("zl", "zh", "x", "core", "par")
SIZES = (4, 2, 4, 2, 8)
SAMPLES = AXES[:4]
LANES = 128


def shift(value, axis, by):
    count = lax.axis_size(axis)
    return lax.ppermute(value, axis, [(i, (i + by) % count) for i in range(count)])


def halves(value):
    high = value.astype(jnp.bfloat16)
    low = (value - high.astype(jnp.float32)).astype(jnp.bfloat16)
    return high, low


def product_kernel(place, left_ref, mine_ref, other_ref, *rest):
    out_ref, left, high, low, right = rest[-5:]
    local = mine_ref.shape[1]
    blocks = left_ref.shape[0]

    @pl.when(pl.program_id(0) == 0)
    def _():
        for g in range(left_ref.shape[2] // LANES):
            lanes = pl.ds(g * LANES, LANES)
            for a in range(blocks):
                left[g, pl.ds(a, local, stride=blocks), :] = left_ref[a, :, lanes]
            high[:, lanes], low[:, lanes] = halves(left[g])

    core = place[2]
    right[pl.ds(pl.multiple_of(core * local, local), local), :] = mine_ref[0]
    right[pl.ds(pl.multiple_of((1 - core) * local, local), local), :] = other_ref[0]
    right_high, right_low = halves(right[...])

    def dot(a, b):
        return lax.dot_general(
            a, b, (((1,), (1,)), ((), ())), preferred_element_type=jnp.float32
        )

    value = dot(high[...], right_low) + dot(low[...], right_high) + dot(high[...], right_high)
    out_ref[...] = value


def product(place, left, mine, other, total):
    blocks, local, params = left.shape
    return pl.pallas_call(
        product_kernel,
        grid_spec=pltpu.PrefetchScalarGridSpec(
            num_scalar_prefetch=1,
            grid=(2,),
            in_specs=[
                pl.BlockSpec((blocks, local, params), lambda j, place: (0, 0, 0)),
                pl.BlockSpec((1, local, params), lambda j, place: (j, 0, 0)),
                pl.BlockSpec((1, local, params), lambda j, place: (j, 0, 0)),
            ]
            + [pl.BlockSpec(memory_space=pl.ANY)] * len(total),
            out_specs=pl.BlockSpec(
                (blocks * local, 2 * local), lambda j, place: (0, place[j])
            ),
            scratch_shapes=[
                pltpu.VMEM((params // LANES, blocks * local, LANES), jnp.float32),
                pltpu.VMEM((blocks * local, params), jnp.bfloat16),
                pltpu.VMEM((blocks * local, params), jnp.bfloat16),
                pltpu.VMEM((2 * local, params), jnp.float32),
            ],
        ),
        out_shape=jax.ShapeDtypeStruct((blocks * local, 16 * local), jnp.float32),
        input_output_aliases={4: 0} if total else {},
        compiler_params=pltpu.CompilerParams(vmem_limit_bytes=24 * 1024 * 1024),
        cost_estimate=pl.CostEstimate(
            flops=2 * 3 * blocks * local * 4 * local * params,
            bytes_accessed=4 * (blocks * local * params + 4 * local * params + blocks * local * 4 * local),
            transcendentals=0,
        ),
    )(place, left, mine, other, *total)


def body(log_derivs, sample_vector):
    local, params = log_derivs.shape
    zh, x, core = (lax.axis_index(name) for name in ("zh", "x", "core"))
    x_count = lax.axis_size("x")
    left = lax.all_gather(log_derivs, "zl")
    partial_value = jnp.dot(
        sample_vector, log_derivs, precision=lax.Precision.HIGHEST, preferred_element_type=jnp.float32
    )
    projected = jnp.sum(lax.all_gather(partial_value, SAMPLES), axis=0)

    far = shift(log_derivs, "zh", 1)
    pair = jnp.stack([log_derivs, far])
    mine = [pair] + [shift(pair, "x", by) for by in (1, 3, 2)]
    other = [shift(value, "core", 1) for value in mine]

    total = ()
    for by, m, o in zip((0, 1, 3, 2), mine, other):
        source = lax.rem(x + x_count - by, x_count)
        place = jnp.stack([zh * x_count + source, (1 - zh) * x_count + source, core]).astype(jnp.int32)
        total = (product(place, left, m, o, total),)
    summed = lax.psum_scatter(total[0], "par", scatter_dimension=0, tiled=True)
    gram_tiles = summed.reshape(-1, left.shape[0], summed.shape[1])
    return (gram_tiles, projected)


def solution(mesh):
    split = Mesh(mesh.devices.reshape(SIZES), AXES)
    in_specs = (P(SAMPLES, "par"), P(SAMPLES))
    out_specs = (P(("zh", "x", "core", "par"), None, "zl"), P("par"))
    return jax.shard_map(body, mesh=split, in_specs=in_specs, out_specs=out_specs, check_vma=False)
```

```python
import jax
import jax.numpy as jnp
from jax import lax
from jax.experimental import pallas as pl
from jax.experimental.pallas import tpu as pltpu
from jax.sharding import Mesh, PartitionSpec as P

AXES = ("zl", "zh", "x", "core", "par")
SIZES = (4, 2, 4, 2, 8)
SAMPLES = AXES[:4]
LANES = 128
PIECE = (4, 3, -3, 2, -2, 1, -1, 0)
HOPS = (0, 1, 3, 2)


def shift(value, axis, by):
    count = lax.axis_size(axis)
    return lax.ppermute(value, axis, [(i, (i + by) % count) for i in range(count)])


def swap(value, axis, bit):
    return lax.ppermute(value, axis, [(i, i ^ bit) for i in range(lax.axis_size(axis))])


def beside(data, value, axis, bit):
    return lax.optimization_barrier((data, value + swap(value, axis, bit)))


def halves(value):
    high = value.astype(jnp.bfloat16)
    low = (value - high.astype(jnp.float32)).astype(jnp.bfloat16)
    return high, low


def product_kernel(place, left_ref, mine_ref, other_ref, *rest):
    outs, (left, high, low, right) = rest[:-4], rest[-4:]
    blocks, local, params = left_ref.shape
    share = local // len(PIECE)
    rows = blocks * share

    @pl.when(pl.program_id(0) == 0)
    def _():
        for g in range(params // LANES):
            lanes = pl.ds(g * LANES, LANES)
            for n in range(len(PIECE)):
                first = pl.multiple_of(place[5 + n] * share, share)
                for a in range(blocks):
                    left[g, pl.ds(n * rows + a, share, stride=blocks), :] = left_ref[
                        a, pl.ds(first, share), lanes
                    ]
            high[:, lanes], low[:, lanes] = halves(left[g])

    core = place[4]
    right[pl.ds(pl.multiple_of(core * local, local), local), :] = mine_ref[0]
    right[pl.ds(pl.multiple_of((1 - core) * local, local), local), :] = other_ref[0]
    right_high, right_low = halves(right[...])

    def dot(a, b):
        return lax.dot_general(
            a, b, (((1,), (1,)), ((), ())), preferred_element_type=jnp.float32
        )

    value = dot(high[...], right_low) + dot(low[...], right_high) + dot(high[...], right_high)
    outs[0][...] = value[: rows // 2]
    outs[1][...] = value[rows // 2 : rows]
    for n in range(1, len(PIECE)):
        outs[n + 1][...] = value[n * rows : (n + 1) * rows]


def product(place, left, mine, other):
    blocks, local, params = left.shape
    count = len(mine)
    rows = blocks * local // len(PIECE)
    heights = (rows // 2,) * 2 + (rows,) * (len(PIECE) - 1)
    return pl.pallas_call(
        product_kernel,
        grid_spec=pltpu.PrefetchScalarGridSpec(
            num_scalar_prefetch=1,
            grid=(count,),
            in_specs=[
                pl.BlockSpec((blocks, local, params), lambda j, place: (0, 0, 0)),
                pl.BlockSpec((1, local, params), lambda j, place: (j, 0, 0)),
                pl.BlockSpec((1, local, params), lambda j, place: (j, 0, 0)),
            ],
            out_specs=[
                pl.BlockSpec((h, 2 * local), lambda j, place: (0, place[j])) for h in heights
            ],
            scratch_shapes=[
                pltpu.VMEM((params // LANES, blocks * local, LANES), jnp.float32),
                pltpu.VMEM((blocks * local, params), jnp.bfloat16),
                pltpu.VMEM((blocks * local, params), jnp.bfloat16),
                pltpu.VMEM((2 * local, params), jnp.float32),
            ],
        ),
        out_shape=[
            jax.ShapeDtypeStruct((h, 2 * local * count), jnp.float32) for h in heights
        ],
        compiler_params=pltpu.CompilerParams(vmem_limit_bytes=24 * 1024 * 1024),
        cost_estimate=pl.CostEstimate(
            flops=2 * 3 * blocks * local * 2 * local * count * params,
            bytes_accessed=4 * (blocks * local * params + 2 * local * count * (params + blocks * local)),
            transcendentals=0,
        ),
    )(place, left, mine, other)


def finish_kernel(place, own_ref, right_ref, left_ref, *rest):
    value = own_ref[...] + (right_ref[...] + left_ref[...])
    rest[-1][...] = value.reshape(rest[-1].shape)


def finish(place, own, from_left, from_right, blocks, done):
    rows, columns = own.shape
    spec = pl.BlockSpec((rows, columns), lambda j, place: (0, 0))
    return pl.pallas_call(
        finish_kernel,
        grid_spec=pltpu.PrefetchScalarGridSpec(
            num_scalar_prefetch=1,
            grid=(1,),
            in_specs=[spec] * 3 + [pl.BlockSpec(memory_space=pl.ANY)] * len(done),
            out_specs=pl.BlockSpec(
                (rows // blocks, blocks, columns), lambda j, place: (0, 0, place[0])
            ),
        ),
        out_shape=jax.ShapeDtypeStruct((rows // blocks, blocks, 2 * columns), jnp.float32),
        input_output_aliases={4: 0} if done else {},
        compiler_params=pltpu.CompilerParams(vmem_limit_bytes=24 * 1024 * 1024),
        cost_estimate=pl.CostEstimate(
            flops=2 * rows * columns, bytes_accessed=16 * rows * columns, transcendentals=0
        ),
    )(place, own, from_left, from_right, *done)


def body(log_derivs, sample_vector):
    zh, x, core, par = (lax.axis_index(name) for name in ("zh", "x", "core", "par"))
    x_count, par_count = lax.axis_size("x"), lax.axis_size("par")
    left = lax.all_gather(log_derivs, "zl")
    blocks = left.shape[0]

    value = jnp.dot(
        sample_vector, log_derivs, precision=lax.Precision.HIGHEST, preferred_element_type=jnp.float32
    )
    far = swap(log_derivs, "zh", 1)
    near = jnp.stack([log_derivs] + [shift(log_derivs, "x", by) for by in HOPS[1:]])
    near, value = beside(near, value, "core", 1)
    near_other = swap(near, "core", 1)
    far, value = beside(far, value, "x", 1)
    far = jnp.stack([far] + [shift(far, "x", by) for by in HOPS[1:]])
    far, value = beside(far, value, "x", 2)
    far_other = swap(far, "core", 1)

    place = jnp.stack(
        [lax.rem(x + x_count - by, x_count) for by in HOPS]
        + [core]
        + [lax.rem(par + par_count + to, par_count) for to in PIECE]
    ).astype(jnp.int32)
    parts = [product(place, left, near, near_other), product(place, left, far, far_other)]

    half = parts[0][0].shape[0]
    going = [[p[0], p[1]] for p in parts]
    for step in range(1, 5):
        arrived = [[shift(g[0], "par", 1), shift(g[1], "par", -1)] for g in going]
        if step < 4:
            arrived, value = beside(arrived, value, *(("zh", 1), ("zl", 1), ("zl", 2))[step - 1])
        if step == 1:
            going = [
                [p[2].at[:half].add(a[0]), p[3].at[half:].add(a[1])] for p, a in zip(parts, arrived)
            ]
        elif step < 4:
            going = [
                [p[2 * step] + a[0], p[2 * step + 1] + a[1]] for p, a in zip(parts, arrived)
            ]
    done = ()
    for part, came, column in zip(parts, arrived, (zh, 1 - zh)):
        done = (finish(column.reshape(1).astype(jnp.int32), part[8], *came, blocks, done),)
    return (done[0], value)


def solution(mesh):
    split = Mesh(mesh.devices.reshape(SIZES), AXES)
    in_specs = (P(SAMPLES, "par"), P(SAMPLES))
    out_specs = (P(("zh", "x", "core", "par"), None, "zl"), P("par"))
    return jax.shard_map(body, mesh=split, in_specs=in_specs, out_specs=out_specs, check_vma=False)
```

```python
import jax
import jax.numpy as jnp
from jax import lax
from jax.experimental import pallas as pl
from jax.experimental.pallas import tpu as pltpu
from jax.sharding import Mesh, PartitionSpec as P

AXES = ("zl", "zh", "x", "core", "par")
SIZES = (4, 2, 4, 2, 8)
SAMPLES = AXES[:4]
LANES = 128
HOPS = (0, 1, 3, 2)
BUTTERFLY = (("core", 1), ("x", 1), ("x", 2), ("zh", 1), ("zl", 1), ("zl", 2))
VMEM = pltpu.CompilerParams(vmem_limit_bytes=24 * 1024 * 1024)


def shift(value, axis, by):
    count = lax.axis_size(axis)
    return lax.ppermute(value, axis, [(i, (i + by) % count) for i in range(count)])


def swap(value, axis, bit):
    return lax.ppermute(value, axis, [(i, i ^ bit) for i in range(lax.axis_size(axis))])


def halves(value):
    high = value.astype(jnp.bfloat16)
    low = (value - high.astype(jnp.float32)).astype(jnp.bfloat16)
    return high, low


def begin_kernel(data_ref, vector_ref, copy_ref, value_ref):
    copy_ref[...] = data_ref[...]
    value_ref[...] = lax.dot_general(
        vector_ref[...],
        data_ref[...],
        (((1,), (0,)), ((), ())),
        precision=lax.Precision.HIGHEST,
        preferred_element_type=jnp.float32,
    )


def begin(data, vector):
    local, params = data.shape
    return pl.pallas_call(
        begin_kernel,
        out_shape=[
            jax.ShapeDtypeStruct(data.shape, jnp.float32),
            jax.ShapeDtypeStruct((1, params), jnp.float32),
        ],
        compiler_params=VMEM,
        cost_estimate=pl.CostEstimate(
            flops=12 * data.size, bytes_accessed=8 * data.size, transcendentals=0
        ),
    )(data, vector.reshape(1, local))


def left_kernel(left_ref, high_ref, low_ref, rows):
    blocks, local, params = left_ref.shape
    for g in range(params // LANES):
        lanes = pl.ds(g * LANES, LANES)
        for a in range(blocks):
            rows[g, pl.ds(a, local, stride=blocks), :] = left_ref[a, :, lanes]
        high_ref[:, lanes], low_ref[:, lanes] = halves(rows[g])


def left_halves(left):
    blocks, local, params = left.shape
    shape = (blocks * local, params)
    return pl.pallas_call(
        left_kernel,
        out_shape=[jax.ShapeDtypeStruct(shape, jnp.bfloat16)] * 2,
        scratch_shapes=[pltpu.VMEM((params // LANES, blocks * local, LANES), jnp.float32)],
        compiler_params=VMEM,
        cost_estimate=pl.CostEstimate(
            flops=4 * left.size, bytes_accessed=8 * left.size, transcendentals=0
        ),
    )(left)


def product_kernel(place, high_ref, low_ref, near_ref, near_other_ref, far_ref, far_other_ref, out_ref, right):
    local = near_ref.shape[1]
    count = pl.num_programs(0) // 2
    core = place[2 * count]

    def gather(mine_ref, other_ref):
        right[pl.ds(pl.multiple_of(core * local, local), local), :] = mine_ref[0]
        right[pl.ds(pl.multiple_of((1 - core) * local, local), local), :] = other_ref[0]

    @pl.when(pl.program_id(0) < count)
    def _():
        gather(near_ref, near_other_ref)

    @pl.when(pl.program_id(0) >= count)
    def _():
        gather(far_ref, far_other_ref)

    high, low = halves(right[...])

    def dot(a, b):
        return lax.dot_general(
            a, b, (((1,), (1,)), ((), ())), preferred_element_type=jnp.float32
        )

    out_ref[...] = dot(high_ref[...], low) + dot(low_ref[...], high) + dot(high_ref[...], high)


def product(place, left, near, near_other, far, far_other):
    rows, params = left[0].shape
    count, local, _ = near.shape
    whole = pl.BlockSpec((rows, params), lambda j, place: (0, 0))
    first = pl.BlockSpec((1, local, params), lambda j, place: (jnp.minimum(j, count - 1), 0, 0))
    second = pl.BlockSpec((1, local, params), lambda j, place: (jnp.maximum(j - count, 0), 0, 0))
    columns = 4 * count * local
    return pl.pallas_call(
        product_kernel,
        grid_spec=pltpu.PrefetchScalarGridSpec(
            num_scalar_prefetch=1,
            grid=(2 * count,),
            in_specs=[whole, whole, first, first, second, second],
            out_specs=pl.BlockSpec((rows, 2 * local), lambda j, place: (0, place[j])),
            scratch_shapes=[pltpu.VMEM((2 * local, params), jnp.float32)],
        ),
        out_shape=jax.ShapeDtypeStruct((rows, columns), jnp.float32),
        compiler_params=pltpu.CompilerParams(vmem_limit_bytes=58 * 1024 * 1024),
        cost_estimate=pl.CostEstimate(
            flops=6 * rows * columns * params,
            bytes_accessed=4 * (rows * params + columns * params + rows * columns),
            transcendentals=0,
        ),
    )(place, *left, near, near_other, far, far_other)


def body(log_derivs, sample_vector):
    zh, x, core = (lax.axis_index(name) for name in ("zh", "x", "core"))
    x_count = lax.axis_size("x")
    left = lax.all_gather(log_derivs, "zl")
    blocks = left.shape[0]

    copy, value = begin(log_derivs, sample_vector)
    far = swap(copy, "zh", 1)
    near = jnp.stack([copy] + [shift(copy, "x", by) for by in HOPS[1:]])
    near_other = swap(near, "core", 1)
    far = jnp.stack([far] + [shift(far, "x", by) for by in HOPS[1:]])
    far_other = swap(far, "core", 1)

    source = [lax.rem(x + x_count - by, x_count) for by in HOPS]
    place = jnp.stack(
        [zh * x_count + s for s in source] + [(1 - zh) * x_count + s for s in source] + [core]
    ).astype(jnp.int32)
    total = product(place, left_halves(left), near, near_other, far, far_other)

    total, value = lax.optimization_barrier((total, value))
    summed = lax.psum_scatter(total, "par", scatter_dimension=0, tiled=True)
    for axis, bit in BUTTERFLY:
        value = value + swap(value, axis, bit)
    return (summed.reshape(-1, blocks, summed.shape[1]), value[0])


def solution(mesh):
    split = Mesh(mesh.devices.reshape(SIZES), AXES)
    in_specs = (P(SAMPLES, "par"), P(SAMPLES))
    out_specs = (P(("zh", "x", "core", "par"), None, "zl"), P("par"))
    return jax.shard_map(body, mesh=split, in_specs=in_specs, out_specs=out_specs, check_vma=False)
```

```python
import functools

import jax
import jax.numpy as jnp
from jax import lax
from jax.experimental import pallas as pl
from jax.experimental.pallas import tpu as pltpu
from jax.sharding import Mesh, PartitionSpec as P

AXES = ("zl", "zh", "x", "core", "par")
SIZES = (4, 2, 4, 2, 8)
SAMPLES = AXES[:4]
LANES = 128
HOPS = (0, 1, 3, 2)
BUTTERFLY = (("core", 1), ("x", 1), ("x", 2), ("zh", 1), ("zl", 1), ("zl", 2))
VMEM = pltpu.CompilerParams(vmem_limit_bytes=24 * 1024 * 1024)


def shift(value, axis, by):
    count = lax.axis_size(axis)
    return lax.ppermute(value, axis, [(i, (i + by) % count) for i in range(count)])


def swap(value, axis, bit):
    return lax.ppermute(value, axis, [(i, i ^ bit) for i in range(lax.axis_size(axis))])


def halves(value):
    high = value.astype(jnp.bfloat16)
    low = (value - high.astype(jnp.float32)).astype(jnp.bfloat16)
    return high, low


def begin_kernel(data_ref, vector_ref, copy_ref, value_ref):
    copy_ref[...] = data_ref[...]
    value_ref[...] = lax.dot_general(
        vector_ref[...],
        data_ref[...],
        (((1,), (0,)), ((), ())),
        precision=lax.Precision.HIGHEST,
        preferred_element_type=jnp.float32,
    )


def begin(data, vector):
    local, params = data.shape
    return pl.pallas_call(
        begin_kernel,
        out_shape=[
            jax.ShapeDtypeStruct(data.shape, jnp.float32),
            jax.ShapeDtypeStruct((1, params), jnp.float32),
        ],
        compiler_params=VMEM,
        cost_estimate=pl.CostEstimate(
            flops=12 * data.size, bytes_accessed=8 * data.size, transcendentals=0
        ),
    )(data, vector.reshape(1, local))


def left_kernel(left_ref, high_ref, low_ref, rows):
    blocks, local, params = left_ref.shape
    for g in range(params // LANES):
        lanes = pl.ds(g * LANES, LANES)
        for a in range(blocks):
            rows[g, pl.ds(a, local, stride=blocks), :] = left_ref[a, :, lanes]
        high_ref[:, lanes], low_ref[:, lanes] = halves(rows[g])


def left_halves(left):
    blocks, local, params = left.shape
    shape = (blocks * local, params)
    return pl.pallas_call(
        left_kernel,
        out_shape=[jax.ShapeDtypeStruct(shape, jnp.bfloat16)] * 2,
        scratch_shapes=[pltpu.VMEM((params // LANES, blocks * local, LANES), jnp.float32)],
        compiler_params=VMEM,
        cost_estimate=pl.CostEstimate(
            flops=4 * left.size, bytes_accessed=8 * left.size, transcendentals=0
        ),
    )(left)


def product_kernel(is_far, high_ref, low_ref, mine_ref, other_ref, *rest):
    out_hbm, right, value, sent = rest[-4:]
    count, local, _ = mine_ref.shape
    x, core = lax.axis_index("x"), lax.axis_index("core")
    half = lax.axis_index("zh")
    if is_far:
        half = 1 - half
    mine = pl.ds(pl.multiple_of(core * local, local), local)
    other = pl.ds(pl.multiple_of((1 - core) * local, local), local)

    def dot(a, b):
        return lax.dot_general(
            a, b, (((1,), (1,)), ((), ())), preferred_element_type=jnp.float32
        )

    copies = []
    for n in range(count):
        right[n % 2, mine, :] = mine_ref[n]
        right[n % 2, other, :] = other_ref[n]
        high, low = halves(right[n % 2])
        value[n] = dot(high_ref[...], low) + dot(low_ref[...], high) + dot(high_ref[...], high)
        source = lax.rem(x + (count - HOPS[n]), count)
        first = pl.multiple_of((half * count + source) * 2 * local, 2 * local)
        copies.append(
            pltpu.make_async_copy(value.at[n], out_hbm.at[:, pl.ds(first, 2 * local)], sent.at[n])
        )
        copies[-1].start()
    for copy in copies:
        copy.wait()


def product(left, mine, other, total):
    rows, params = left[0].shape
    count, local, _ = mine.shape
    columns = 4 * count * local
    whole = pl.BlockSpec(memory_space=pltpu.VMEM)
    hbm = pl.BlockSpec(memory_space=pltpu.HBM)
    return pl.pallas_call(
        functools.partial(product_kernel, bool(total)),
        in_specs=[whole] * 4 + [hbm] * len(total),
        out_specs=hbm,
        out_shape=pltpu.HBM((rows, columns), jnp.float32),
        input_output_aliases={4: 0} if total else {},
        scratch_shapes=[
            pltpu.VMEM((2, 2 * local, params), jnp.float32),
            pltpu.VMEM((count, rows, 2 * local), jnp.float32),
            pltpu.SemaphoreType.DMA((count,)),
        ],
        compiler_params=VMEM,
        cost_estimate=pl.CostEstimate(
            flops=3 * rows * columns * params,
            bytes_accessed=2 * (rows * params + columns * params + rows * columns),
            transcendentals=0,
        ),
    )(*left, mine, other, *total)


def body(log_derivs, sample_vector):
    left = lax.all_gather(log_derivs, "zl")
    blocks = left.shape[0]

    copy, value = begin(log_derivs, sample_vector)
    far = swap(copy, "zh", 1)
    near = jnp.stack([copy] + [shift(copy, "x", by) for by in HOPS[1:]])
    near_other = swap(near, "core", 1)
    far = jnp.stack([far] + [shift(far, "x", by) for by in HOPS[1:]])
    far, left = lax.optimization_barrier((far, left))
    far_other = swap(far, "core", 1)

    left = left_halves(left)
    total = product(left, near, near_other, ())
    total = product(left, far, far_other, (total,))

    total, value = lax.optimization_barrier((total, value))
    summed = lax.psum_scatter(total, "par", scatter_dimension=0, tiled=True)
    for axis, bit in BUTTERFLY:
        value = value + swap(value, axis, bit)
    return (summed.reshape(-1, blocks, summed.shape[1]), value[0])


def solution(mesh):
    split = Mesh(mesh.devices.reshape(SIZES), AXES)
    in_specs = (P(SAMPLES, "par"), P(SAMPLES))
    out_specs = (P(("zh", "x", "core", "par"), None, "zl"), P("par"))
    return jax.shard_map(body, mesh=split, in_specs=in_specs, out_specs=out_specs, check_vma=False)
```

```python
import functools

import jax
import jax.numpy as jnp
from jax import lax
from jax.experimental import pallas as pl
from jax.experimental.pallas import tpu as pltpu
from jax.sharding import Mesh, PartitionSpec as P

AXES = ("zl", "zh", "x", "core", "par")
SIZES = (4, 2, 4, 2, 8)
SAMPLES = AXES[:4]
LANES = 128
EXTRA = 8
HOPS = (0, 1, 3, 2)
PLACES = (4, 3, -3, 2, -2, 1, -1, 0)
STEPPED = 3
VMEM = pltpu.CompilerParams(vmem_limit_bytes=24 * 1024 * 1024)
IN_VMEM = pl.BlockSpec(memory_space=pltpu.VMEM)
IN_HBM = pl.BlockSpec(memory_space=pltpu.HBM)


def shift(value, axis, by):
    count = lax.axis_size(axis)
    return lax.ppermute(value, axis, [(i, (i + by) % count) for i in range(count)])


def swap(value, axis, bit):
    return lax.ppermute(value, axis, [(i, i ^ bit) for i in range(lax.axis_size(axis))])


def cost(flops, elements):
    return pl.CostEstimate(flops=flops, bytes_accessed=4 * elements, transcendentals=0)


def halves(value):
    high = value.astype(jnp.bfloat16)
    low = (value - high.astype(jnp.float32)).astype(jnp.bfloat16)
    return high, low


def begin_kernel(data_ref, vector_ref, out_ref):
    local, params = data_ref.shape
    out_ref[:local, :] = data_ref[...]
    term = lax.dot_general(
        vector_ref[...],
        data_ref[...],
        (((1,), (0,)), ((), ())),
        precision=lax.Precision.HIGHEST,
        preferred_element_type=jnp.float32,
    )
    out_ref[local:, :] = jnp.broadcast_to(term, (EXTRA, params))


def begin(data, vector):
    local, params = data.shape
    return pl.pallas_call(
        begin_kernel,
        out_shape=jax.ShapeDtypeStruct((local + EXTRA, params), jnp.float32),
        compiler_params=VMEM,
        cost_estimate=cost(12 * data.size, 2 * data.size),
    )(data, vector.reshape(1, local))


def left_kernel(left_ref, high_ref, low_ref, rows):
    blocks, local, params = left_ref.shape
    for g in range(params // LANES):
        lanes = pl.ds(g * LANES, LANES)
        for a in range(blocks):
            rows[g, pl.ds(a, local, stride=blocks), :] = left_ref[a, :, lanes]
        high_ref[:, lanes], low_ref[:, lanes] = halves(rows[g])


def left_halves(left):
    blocks, local, params = left.shape
    shape = (blocks * local, params)
    return pl.pallas_call(
        left_kernel,
        out_shape=[jax.ShapeDtypeStruct(shape, jnp.bfloat16)] * 2,
        scratch_shapes=[pltpu.VMEM((params // LANES, blocks * local, LANES), jnp.float32)],
        compiler_params=VMEM,
        cost_estimate=cost(4 * left.size, 2 * left.size),
    )(left)


def block_product(high_ref, low_ref, mine_ref, other_ref, n, right):
    local = right.shape[0] // 2
    core = lax.axis_index("core")
    right[pl.ds(pl.multiple_of(core * local, local), local), :] = mine_ref[n, :local, :]
    right[pl.ds(pl.multiple_of((1 - core) * local, local), local), :] = other_ref[n, :local, :]
    high, low = halves(right[...])

    def dot(a, b):
        return lax.dot_general(
            a, b, (((1,), (1,)), ((), ())), preferred_element_type=jnp.float32
        )

    return dot(high_ref[...], low) + dot(low_ref[...], high) + dot(high_ref[...], high)


def product_kernel(high_ref, low_ref, near_ref, near_other_ref, far_ref, far_other_ref, *rest):
    (*outs, total_hbm, term_ref), (right, value, steps, sent) = rest[:-4], rest[-4:]
    count, places = near_ref.shape[0], len(PLACES)
    local = near_ref.shape[1] - EXTRA
    width = value.shape[2]
    copies = []
    for m, n in enumerate(range(STEPPED, 2 * count)):
        pair = (near_ref, near_other_ref) if n < count else (far_ref, far_other_ref)
        value[m] = block_product(high_ref, low_ref, *pair, n % count, right.at[m % 2])
        copies.append(
            pltpu.make_async_copy(
                value.at[m], total_hbm.at[:, pl.ds(m * width, width)], sent.at[m]
            )
        )
        copies[-1].start()

    for n in range(STEPPED):
        steps[:, n * width : (n + 1) * width] = block_product(
            high_ref, low_ref, near_ref, near_other_ref, n, right.at[n % 2]
        )
    par = lax.axis_index("par")
    rows = steps.shape[0] // places
    for n, to in enumerate(PLACES):
        first = pl.multiple_of(lax.rem(par + (places + to), places) * rows, rows)
        if n:
            outs[n + 1][...] = steps[pl.ds(first, rows), :]
        else:
            outs[0][...] = steps[pl.ds(first, rows // 2), :]
            outs[1][...] = steps[pl.ds(pl.multiple_of(first + rows // 2, rows // 2), rows // 2), :]

    def pairs(ref):
        row = [ref[HOPS.index(by), pl.ds(local, 1), :] for by in range(count)]
        return (row[0] + row[2]) + (row[1] + row[3])

    near_term = pairs(near_ref) + pairs(near_other_ref)
    far_term = pairs(far_ref) + pairs(far_other_ref)
    term_ref[...] = near_term + far_term
    for copy in copies:
        copy.wait()


def product(left, near, near_other, far, far_other):
    total_rows, params = left[0].shape
    count, height, _ = near.shape
    width = 2 * (height - EXTRA)
    blocks = 2 * count - STEPPED
    rows = total_rows // len(PLACES)
    heights = (rows // 2,) * 2 + (rows,) * (len(PLACES) - 1)
    *parts, total, term = pl.pallas_call(
        product_kernel,
        in_specs=[IN_VMEM] * 6,
        out_specs=[IN_VMEM] * len(heights) + [IN_HBM, IN_VMEM],
        out_shape=[jax.ShapeDtypeStruct((h, STEPPED * width), jnp.float32) for h in heights]
        + [
            pltpu.HBM((total_rows, blocks * width), jnp.float32),
            jax.ShapeDtypeStruct((1, params), jnp.float32),
        ],
        scratch_shapes=[
            pltpu.VMEM((2, width, params), jnp.float32),
            pltpu.VMEM((blocks, total_rows, width), jnp.float32),
            pltpu.VMEM((total_rows, STEPPED * width), jnp.float32),
            pltpu.SemaphoreType.DMA((blocks,)),
        ],
        compiler_params=VMEM,
        cost_estimate=cost(12 * total_rows * count * width * params, 2 * count * width * (params + total_rows)),
    )(*left, near, near_other, far, far_other)
    return parts, total, term


def write_kernel(first_block, *rest):
    out_hbm, value, sent = rest[-3:]
    terms = rest[:-3][: 3 if first_block == 0 else 1]
    count = len(HOPS)
    x, zh = lax.axis_index("x"), lax.axis_index("zh")
    blocks, _, _, width = value.shape
    copies = []
    for m in range(blocks):
        columns = pl.ds(m * width, width)
        total = terms[0][:, columns]
        if len(terms) == 3:
            total = total + (terms[1][:, columns] + terms[2][:, columns])
        value[m] = total.reshape(value.shape[1:])
        n = first_block + m
        half = zh if n < count else 1 - zh
        source = lax.rem(x + (count - HOPS[n % count]), count)
        first = pl.multiple_of((half * count + source) * width, width)
        copies.append(
            pltpu.make_async_copy(value.at[m], out_hbm.at[:, :, pl.ds(first, width)], sent.at[m])
        )
        copies[-1].start()
    for copy in copies:
        copy.wait()


def write(first_block, terms, width, blocks, done):
    rows, columns = terms[0].shape
    shape = (rows // blocks, blocks)
    return pl.pallas_call(
        functools.partial(write_kernel, first_block),
        in_specs=[IN_VMEM] * len(terms) + [IN_HBM] * len(done),
        out_specs=IN_HBM,
        out_shape=pltpu.HBM(shape + (2 * len(HOPS) * width,), jnp.float32),
        input_output_aliases={len(terms): 0} if done else {},
        scratch_shapes=[
            pltpu.VMEM((columns // width,) + shape + (width,), jnp.float32),
            pltpu.SemaphoreType.DMA((columns // width,)),
        ],
        compiler_params=VMEM,
        cost_estimate=cost(2 * rows * columns, (len(terms) + 1) * rows * columns),
    )(*terms, *done)


def body(log_derivs, sample_vector):
    left = lax.all_gather(log_derivs, "zl")
    blocks, local, _ = left.shape

    own = begin(log_derivs, sample_vector)
    far = swap(own, "zh", 1)
    near = jnp.stack([own] + [shift(own, "x", by) for by in HOPS[1:]])
    near_other = swap(near, "core", 1)
    far = jnp.stack([far] + [shift(far, "x", by) for by in HOPS[1:]])
    far, left = lax.optimization_barrier((far, left))
    far_other = swap(far, "core", 1)

    left = left_halves(left)
    parts, total, value = product(left, near, near_other, far, far_other)
    summed = lax.psum_scatter(total, "par", scatter_dimension=0, tiled=True)
    half = parts[0].shape[0]
    going = [parts[0], parts[1]]
    for step in range(1, 5):
        came = [shift(going[0], "par", 1), shift(going[1], "par", -1)]
        if step in (2, 3):
            value = value + swap(value, "zl", step - 1)
            came, value = lax.optimization_barrier((came, value))
        if step == 1:
            going = [parts[2].at[:half].add(came[0]), parts[3].at[half:].add(came[1])]
        elif step < 4:
            going = [parts[2 * step] + came[0], parts[2 * step + 1] + came[1]]
    done = write(0, [parts[8]] + came, 2 * local, blocks, ())
    summed, done = lax.optimization_barrier((summed, done))
    return (write(STEPPED, [summed], 2 * local, blocks, (done,)), value[0])


def solution(mesh):
    split = Mesh(mesh.devices.reshape(SIZES), AXES)
    in_specs = (P(SAMPLES, "par"), P(SAMPLES))
    out_specs = (P(("zh", "x", "core", "par"), None, "zl"), P("par"))
    return jax.shard_map(body, mesh=split, in_specs=in_specs, out_specs=out_specs, check_vma=False)
```

```python
import jax
import jax.numpy as jnp
from jax import lax
from jax.experimental import pallas as pl
from jax.experimental.pallas import tpu as pltpu
from jax.sharding import Mesh, PartitionSpec as P

AXES = ("zl", "zh", "x", "core", "par")
SIZES = (4, 2, 4, 2, 8)
SAMPLES = AXES[:4]
LANES = 128
EXTRA = 8
HOPS = (0, 1, 3, 2)
VMEM = pltpu.CompilerParams(vmem_limit_bytes=24 * 1024 * 1024)
IN_VMEM = pl.BlockSpec(memory_space=pltpu.VMEM)
IN_HBM = pl.BlockSpec(memory_space=pltpu.HBM)


def shift(value, axis, by):
    count = lax.axis_size(axis)
    return lax.ppermute(value, axis, [(i, (i + by) % count) for i in range(count)])


def swap(value, axis, bit):
    return lax.ppermute(value, axis, [(i, i ^ bit) for i in range(lax.axis_size(axis))])


def cost(flops, elements):
    return pl.CostEstimate(flops=flops, bytes_accessed=4 * elements, transcendentals=0)


def halves(value):
    high = value.astype(jnp.bfloat16)
    low = (value - high.astype(jnp.float32)).astype(jnp.bfloat16)
    return high, low


def begin_kernel(data_ref, vector_ref, out_ref):
    local, params = data_ref.shape
    out_ref[:local, :] = data_ref[...]
    term = lax.dot_general(
        vector_ref[...],
        data_ref[...],
        (((1,), (0,)), ((), ())),
        precision=lax.Precision.HIGHEST,
        preferred_element_type=jnp.float32,
    )
    out_ref[local:, :] = jnp.broadcast_to(term, (EXTRA, params))


def begin(data, vector):
    local, params = data.shape
    return pl.pallas_call(
        begin_kernel,
        out_shape=jax.ShapeDtypeStruct((local + EXTRA, params), jnp.float32),
        compiler_params=VMEM,
        cost_estimate=cost(12 * data.size, 2 * data.size),
    )(data, vector.reshape(1, local))


def left_kernel(left_ref, high_ref, low_ref, rows):
    blocks, local, params = left_ref.shape
    for g in range(params // LANES):
        lanes = pl.ds(g * LANES, LANES)
        for a in range(blocks):
            rows[g, pl.ds(a, local, stride=blocks), :] = left_ref[a, :, lanes]
        high_ref[:, lanes], low_ref[:, lanes] = halves(rows[g])


def left_halves(left):
    blocks, local, params = left.shape
    shape = (blocks * local, params)
    return pl.pallas_call(
        left_kernel,
        out_shape=[jax.ShapeDtypeStruct(shape, jnp.bfloat16)] * 2,
        scratch_shapes=[pltpu.VMEM((params // LANES, blocks * local, LANES), jnp.float32)],
        compiler_params=VMEM,
        cost_estimate=cost(4 * left.size, 2 * left.size),
    )(left)


def block_product(high_ref, low_ref, mine_ref, other_ref, n, right):
    local = right.shape[0] // 2
    core = lax.axis_index("core")
    right[pl.ds(pl.multiple_of(core * local, local), local), :] = mine_ref[n, :local, :]
    right[pl.ds(pl.multiple_of((1 - core) * local, local), local), :] = other_ref[n, :local, :]
    high, low = halves(right[...])

    def dot(a, b):
        return lax.dot_general(
            a, b, (((1,), (1,)), ((), ())), preferred_element_type=jnp.float32
        )

    return dot(high_ref[...], low) + dot(low_ref[...], high) + dot(high_ref[...], high)


def product_kernel(high_ref, low_ref, near_ref, near_other_ref, far_ref, far_other_ref, total_hbm, term_ref, right, value, sent):
    count = near_ref.shape[0]
    local = near_ref.shape[1] - EXTRA
    width = value.shape[2]
    copies = []
    for n in range(2 * count):
        pair = (near_ref, near_other_ref) if n < count else (far_ref, far_other_ref)
        value[n] = block_product(high_ref, low_ref, *pair, n % count, right.at[n % 2])
        copies.append(
            pltpu.make_async_copy(
                value.at[n], total_hbm.at[:, pl.ds(n * width, width)], sent.at[n]
            )
        )
        copies[-1].start()

    def pairs(ref):
        row = [ref[HOPS.index(by), pl.ds(local, 1), :] for by in range(count)]
        return (row[0] + row[2]) + (row[1] + row[3])

    near_term = pairs(near_ref) + pairs(near_other_ref)
    far_term = pairs(far_ref) + pairs(far_other_ref)
    term_ref[...] = near_term + far_term
    for copy in copies:
        copy.wait()


def product(left, near, near_other, far, far_other):
    rows, params = left[0].shape
    count, height, _ = near.shape
    width = 2 * (height - EXTRA)
    blocks = 2 * count
    return pl.pallas_call(
        product_kernel,
        in_specs=[IN_VMEM] * 6,
        out_specs=[IN_HBM, IN_VMEM],
        out_shape=[
            pltpu.HBM((rows, blocks * width), jnp.float32),
            jax.ShapeDtypeStruct((1, params), jnp.float32),
        ],
        scratch_shapes=[
            pltpu.VMEM((2, width, params), jnp.float32),
            pltpu.VMEM((blocks, rows, width), jnp.float32),
            pltpu.SemaphoreType.DMA((blocks,)),
        ],
        compiler_params=VMEM,
        cost_estimate=cost(6 * rows * blocks * width * params, blocks * width * (params + rows)),
    )(*left, near, near_other, far, far_other)


def write_kernel(sum_ref, out_hbm, value, sent):
    count = len(HOPS)
    x, zh = lax.axis_index("x"), lax.axis_index("zh")
    blocks, _, _, width = value.shape
    copies = []
    for n in range(blocks):
        value[n] = sum_ref[:, pl.ds(n * width, width)].reshape(value.shape[1:])
        half = zh if n < count else 1 - zh
        source = lax.rem(x + (count - HOPS[n % count]), count)
        first = pl.multiple_of((half * count + source) * width, width)
        copies.append(
            pltpu.make_async_copy(value.at[n], out_hbm.at[:, :, pl.ds(first, width)], sent.at[n])
        )
        copies[-1].start()
    for copy in copies:
        copy.wait()


def write(summed, blocks):
    rows, columns = summed.shape
    count = 2 * len(HOPS)
    shape = (rows // blocks, blocks)
    return pl.pallas_call(
        write_kernel,
        in_specs=[IN_VMEM],
        out_specs=IN_HBM,
        out_shape=pltpu.HBM(shape + (columns,), jnp.float32),
        scratch_shapes=[
            pltpu.VMEM((count,) + shape + (columns // count,), jnp.float32),
            pltpu.SemaphoreType.DMA((count,)),
        ],
        compiler_params=VMEM,
        cost_estimate=cost(0, 2 * rows * columns),
    )(summed)


def body(log_derivs, sample_vector):
    left = lax.all_gather(log_derivs, "zl")
    blocks = left.shape[0]

    own = begin(log_derivs, sample_vector)
    far = swap(own, "zh", 1)
    near = jnp.stack([own] + [shift(own, "x", by) for by in HOPS[1:]])
    near_other = swap(near, "core", 1)
    far = jnp.stack([far] + [shift(far, "x", by) for by in HOPS[1:]])
    far, left = lax.optimization_barrier((far, left))
    far_other = swap(far, "core", 1)

    left = left_halves(left)
    total, value = product(left, near, near_other, far, far_other)
    summed = lax.psum_scatter(total, "par", scatter_dimension=0, tiled=True)
    for bit in (1, 2):
        value = value + swap(value, "zl", bit)
    return (write(summed, blocks), value[0])


def solution(mesh):
    split = Mesh(mesh.devices.reshape(SIZES), AXES)
    in_specs = (P(SAMPLES, "par"), P(SAMPLES))
    out_specs = (P(("zh", "x", "core", "par"), None, "zl"), P("par"))
    return jax.shard_map(body, mesh=split, in_specs=in_specs, out_specs=out_specs, check_vma=False)
```

```python
import jax
import jax.numpy as jnp
from jax import lax
from jax.experimental import pallas as pl
from jax.experimental.pallas import tpu as pltpu
from jax.sharding import Mesh, PartitionSpec as P

AXES = ("zl", "zh", "x", "core", "par")
SIZES = (4, 2, 4, 2, 8)
SAMPLES = AXES[:4]
LANES = 128
HOPS = (0, 1, 3, 2)
BUTTERFLY = (("core", 1), ("x", 1), ("x", 2), ("zh", 1), ("zl", 1), ("zl", 2))
VMEM = pltpu.CompilerParams(vmem_limit_bytes=24 * 1024 * 1024)


def shift(value, axis, by):
    count = lax.axis_size(axis)
    return lax.ppermute(value, axis, [(i, (i + by) % count) for i in range(count)])


def swap(value, axis, bit):
    return lax.ppermute(value, axis, [(i, i ^ bit) for i in range(lax.axis_size(axis))])


def halves(value):
    high = value.astype(jnp.bfloat16)
    low = (value - high.astype(jnp.float32)).astype(jnp.bfloat16)
    return high, low


def term_kernel(data_ref, vector_ref, term_ref):
    term_ref[...] = lax.dot_general(
        vector_ref[...],
        data_ref[...],
        (((1,), (0,)), ((), ())),
        precision=lax.Precision.HIGHEST,
        preferred_element_type=jnp.float32,
    )


def term(data, vector):
    local, params = data.shape
    return pl.pallas_call(
        term_kernel,
        out_shape=jax.ShapeDtypeStruct((1, params), jnp.float32),
        compiler_params=VMEM,
        cost_estimate=pl.CostEstimate(
            flops=12 * data.size, bytes_accessed=4 * data.size, transcendentals=0
        ),
    )(data, vector.reshape(1, local))


def left_kernel(left_ref, high_ref, low_ref, rows):
    blocks, local, params = left_ref.shape
    for g in range(params // LANES):
        lanes = pl.ds(g * LANES, LANES)
        for a in range(blocks):
            rows[g, pl.ds(a, local, stride=blocks), :] = left_ref[a, :, lanes]
        high_ref[:, lanes], low_ref[:, lanes] = halves(rows[g])


def left_halves(left):
    blocks, local, params = left.shape
    shape = (blocks * local, params)
    return pl.pallas_call(
        left_kernel,
        out_shape=[jax.ShapeDtypeStruct(shape, jnp.bfloat16)] * 2,
        scratch_shapes=[pltpu.VMEM((params // LANES, blocks * local, LANES), jnp.float32)],
        compiler_params=VMEM,
        cost_estimate=pl.CostEstimate(
            flops=4 * left.size, bytes_accessed=8 * left.size, transcendentals=0
        ),
    )(left)


def multiply(high_ref, low_ref, mine_ref, other_ref, n, right):
    local = mine_ref.shape[1]
    core = lax.axis_index("core")
    right[pl.ds(pl.multiple_of(core * local, local), local), :] = mine_ref[n]
    right[pl.ds(pl.multiple_of((1 - core) * local, local), local), :] = other_ref[n]
    high, low = halves(right[...])

    def dot(a, b):
        return lax.dot_general(
            a, b, (((1,), (1,)), ((), ())), preferred_element_type=jnp.float32
        )

    return dot(high_ref[...], low) + dot(low_ref[...], high) + dot(high_ref[...], high)


def near_kernel(high_ref, low_ref, mine_ref, other_ref, out_ref, right):
    for n in range(out_ref.shape[0]):
        out_ref[n] = multiply(high_ref, low_ref, mine_ref, other_ref, n, right.at[n % 2])


def far_kernel(near_value, high_ref, low_ref, mine_ref, other_ref, total_hbm, far_value, right, sent):
    count, _, width = far_value.shape
    x, zh = lax.axis_index("x"), lax.axis_index("zh")

    def send(value, half, n):
        source = lax.rem(x + (count - HOPS[n % count]), count)
        first = pl.multiple_of((half * count + source) * width, width)
        return pltpu.make_async_copy(
            value.at[n % count], total_hbm.at[:, pl.ds(first, width)], sent.at[n]
        )

    copies = [send(near_value, zh, n) for n in range(count)]
    for copy in copies:
        copy.start()
    for n in range(count):
        far_value[n] = multiply(high_ref, low_ref, mine_ref, other_ref, n, right.at[n % 2])
        copies.append(send(far_value, 1 - zh, count + n))
        copies[-1].start()
    for copy in copies:
        copy.wait()


def product(left, near, near_other, far, far_other):
    rows, params = left[0].shape
    count, local, _ = near.shape
    width = 2 * local
    whole = pl.BlockSpec(memory_space=pltpu.VMEM)
    value = (count, rows, width)
    right = pltpu.VMEM((2, width, params), jnp.float32)
    cost = pl.CostEstimate(
        flops=6 * rows * count * width * params,
        bytes_accessed=4 * count * width * (params + rows),
        transcendentals=0,
    )
    near_value = pl.pallas_call(
        near_kernel,
        in_specs=[whole] * 4,
        out_specs=whole,
        out_shape=jax.ShapeDtypeStruct(value, jnp.float32),
        scratch_shapes=[right],
        compiler_params=VMEM,
        cost_estimate=cost,
    )(*left, near, near_other)
    return pl.pallas_call(
        far_kernel,
        in_specs=[whole] * 5,
        out_specs=pl.BlockSpec(memory_space=pltpu.HBM),
        out_shape=pltpu.HBM((rows, 2 * count * width), jnp.float32),
        scratch_shapes=[pltpu.VMEM(value, jnp.float32), right, pltpu.SemaphoreType.DMA((2 * count,))],
        compiler_params=VMEM,
        cost_estimate=cost,
    )(near_value, *left, far, far_other)


def body(log_derivs, sample_vector):
    left = lax.all_gather(log_derivs, "zl")
    blocks = left.shape[0]

    far = swap(log_derivs, "zh", 1)
    near = jnp.stack([log_derivs] + [shift(log_derivs, "x", by) for by in HOPS[1:]])
    near_other = swap(near, "core", 1)
    far = jnp.stack([far] + [shift(far, "x", by) for by in HOPS[1:]])
    far, left = lax.optimization_barrier((far, left))
    far_other = swap(far, "core", 1)

    total = product(left_halves(left), near, near_other, far, far_other)
    total, log_derivs, sample_vector = lax.optimization_barrier((total, log_derivs, sample_vector))
    summed = lax.psum_scatter(total, "par", scatter_dimension=0, tiled=True)
    value = term(log_derivs, sample_vector)
    for axis, bit in BUTTERFLY:
        value = value + swap(value, axis, bit)
    return (summed.reshape(-1, blocks, summed.shape[1]), value[0])


def solution(mesh):
    split = Mesh(mesh.devices.reshape(SIZES), AXES)
    in_specs = (P(SAMPLES, "par"), P(SAMPLES))
    out_specs = (P(("zh", "x", "core", "par"), None, "zl"), P("par"))
    return jax.shard_map(body, mesh=split, in_specs=in_specs, out_specs=out_specs, check_vma=False)
```

```python
import jax
import jax.numpy as jnp
from jax import lax
from jax.experimental import pallas as pl
from jax.experimental.pallas import tpu as pltpu
from jax.sharding import Mesh, PartitionSpec as P

AXES = ("zl", "zh", "x", "core", "par")
SIZES = (4, 2, 4, 2, 8)
SAMPLES = AXES[:4]
LANES = 128
PARTS = 4
HOPS = (0, 1, 3, 2)
BUTTERFLY = (("core", 1), ("x", 1), ("x", 2), ("zh", 1), ("zl", 1), ("zl", 2))
VMEM = pltpu.CompilerParams(vmem_limit_bytes=24 * 1024 * 1024)


def shift(value, axis, by):
    count = lax.axis_size(axis)
    return lax.ppermute(value, axis, [(i, (i + by) % count) for i in range(count)])


def swap(value, axis, bit):
    return lax.ppermute(value, axis, [(i, i ^ bit) for i in range(lax.axis_size(axis))])


def halves(value):
    high = value.astype(jnp.bfloat16)
    low = (value - high.astype(jnp.float32)).astype(jnp.bfloat16)
    return high, low


def term_kernel(data_ref, vector_ref, term_ref):
    term_ref[...] = lax.dot_general(
        vector_ref[...],
        data_ref[...],
        (((1,), (0,)), ((), ())),
        precision=lax.Precision.HIGHEST,
        preferred_element_type=jnp.float32,
    )


def term(data, vector):
    local, params = data.shape
    return pl.pallas_call(
        term_kernel,
        out_shape=jax.ShapeDtypeStruct((1, params), jnp.float32),
        compiler_params=VMEM,
        cost_estimate=pl.CostEstimate(
            flops=12 * data.size, bytes_accessed=4 * data.size, transcendentals=0
        ),
    )(data, vector.reshape(1, local))


def left_kernel(left_ref, high_ref, low_ref, rows):
    blocks, local, params = left_ref.shape
    for g in range(params // LANES):
        lanes = pl.ds(g * LANES, LANES)
        for a in range(blocks):
            rows[g, pl.ds(a, local, stride=blocks), :] = left_ref[a, :, lanes]
        high_ref[:, lanes], low_ref[:, lanes] = halves(rows[g])


def left_halves(left):
    blocks, local, params = left.shape
    shape = (blocks * local, params)
    return pl.pallas_call(
        left_kernel,
        out_shape=[jax.ShapeDtypeStruct(shape, jnp.bfloat16)] * 2,
        scratch_shapes=[pltpu.VMEM((params // LANES, blocks * local, LANES), jnp.float32)],
        compiler_params=VMEM,
        cost_estimate=pl.CostEstimate(
            flops=4 * left.size, bytes_accessed=8 * left.size, transcendentals=0
        ),
    )(left)


def multiply(high_ref, low_ref, mine_ref, other_ref, n, right):
    local = mine_ref.shape[1]
    core = lax.axis_index("core")
    right[pl.ds(pl.multiple_of(core * local, local), local), :] = mine_ref[n]
    right[pl.ds(pl.multiple_of((1 - core) * local, local), local), :] = other_ref[n]
    high, low = halves(right[...])

    def dot(a, b):
        return lax.dot_general(
            a, b, (((1,), (1,)), ((), ())), preferred_element_type=jnp.float32
        )

    return dot(high_ref[...], low) + dot(low_ref[...], high) + dot(high_ref[...], high)


def near_kernel(high_ref, low_ref, mine_ref, other_ref, out_ref, right):
    for n in range(out_ref.shape[0]):
        out_ref[n] = multiply(high_ref, low_ref, mine_ref, other_ref, n, right.at[n % 2])


def far_kernel(near_value, high_ref, low_ref, mine_ref, other_ref, total_hbm, far_value, right, sent):
    count, rows, width = far_value.shape
    x, zh = lax.axis_index("x"), lax.axis_index("zh")

    def send(value, half, n):
        source = lax.rem(x + (count - HOPS[n % count]), count)
        first = pl.multiple_of((half * count + source) * width, width)
        for part in range(PARTS):
            some = pl.ds(part * (rows // PARTS), rows // PARTS)
            copies.append(
                pltpu.make_async_copy(
                    value.at[n % count, some, :],
                    total_hbm.at[some, pl.ds(first, width)],
                    sent.at[n, part],
                )
            )
            copies[-1].start()

    copies = []
    for n in range(count):
        send(near_value, zh, n)
    for n in range(count):
        far_value[n] = multiply(high_ref, low_ref, mine_ref, other_ref, n, right.at[n % 2])
        send(far_value, 1 - zh, count + n)
    for copy in copies:
        copy.wait()


def product(left, near, near_other, far, far_other):
    rows, params = left[0].shape
    count, local, _ = near.shape
    width = 2 * local
    whole = pl.BlockSpec(memory_space=pltpu.VMEM)
    value = (count, rows, width)
    right = pltpu.VMEM((2, width, params), jnp.float32)
    cost = pl.CostEstimate(
        flops=6 * rows * count * width * params,
        bytes_accessed=4 * count * width * (params + rows),
        transcendentals=0,
    )
    near_value = pl.pallas_call(
        near_kernel,
        in_specs=[whole] * 4,
        out_specs=whole,
        out_shape=jax.ShapeDtypeStruct(value, jnp.float32),
        scratch_shapes=[right],
        compiler_params=VMEM,
        cost_estimate=cost,
    )(*left, near, near_other)
    return pl.pallas_call(
        far_kernel,
        in_specs=[whole] * 5,
        out_specs=pl.BlockSpec(memory_space=pltpu.HBM),
        out_shape=pltpu.HBM((rows, 2 * count * width), jnp.float32),
        scratch_shapes=[pltpu.VMEM(value, jnp.float32), right, pltpu.SemaphoreType.DMA((2 * count, PARTS))],
        compiler_params=VMEM,
        cost_estimate=cost,
    )(near_value, *left, far, far_other)


def write_kernel(sum_hbm, out_hbm, summed, value, arrived, sent):
    parts, rows, _ = summed.shape
    lines = value.shape[1]
    copies = [
        pltpu.make_async_copy(sum_hbm.at[pl.ds(n * rows, rows), :], summed.at[n], arrived.at[n])
        for n in range(parts)
    ]
    for copy in copies:
        copy.start()
    leaving = []
    for n in range(parts):
        copies[n].wait()
        value[n] = summed[n].reshape(value.shape[1:])
        leaving.append(
            pltpu.make_async_copy(value.at[n], out_hbm.at[pl.ds(n * lines, lines)], sent.at[n])
        )
        leaving[-1].start()
    for copy in leaving:
        copy.wait()


def write(summed, blocks):
    rows, columns = summed.shape
    hbm = pl.BlockSpec(memory_space=pltpu.HBM)
    return pl.pallas_call(
        write_kernel,
        in_specs=[hbm],
        out_specs=hbm,
        out_shape=pltpu.HBM((rows // blocks, blocks, columns), jnp.float32),
        scratch_shapes=[
            pltpu.VMEM((PARTS, rows // PARTS, columns), jnp.float32),
            pltpu.VMEM((PARTS, rows // PARTS // blocks, blocks, columns), jnp.float32),
            pltpu.SemaphoreType.DMA((PARTS,)),
            pltpu.SemaphoreType.DMA((PARTS,)),
        ],
        compiler_params=pltpu.CompilerParams(vmem_limit_bytes=60 * 1024 * 1024),
        cost_estimate=pl.CostEstimate(flops=0, bytes_accessed=8 * summed.size, transcendentals=0),
    )(summed)


def body(log_derivs, sample_vector):
    left = lax.all_gather(log_derivs, "zl")
    blocks = left.shape[0]

    far = swap(log_derivs, "zh", 1)
    near = jnp.stack([log_derivs] + [shift(log_derivs, "x", by) for by in HOPS[1:]])
    near_other = swap(near, "core", 1)
    far = jnp.stack([far] + [shift(far, "x", by) for by in HOPS[1:]])
    far, left = lax.optimization_barrier((far, left))
    far_other = swap(far, "core", 1)

    total = product(left_halves(left), near, near_other, far, far_other)
    total, log_derivs, sample_vector = lax.optimization_barrier((total, log_derivs, sample_vector))
    summed = lax.psum_scatter(total, "par", scatter_dimension=0, tiled=True)
    value = term(log_derivs, sample_vector)
    for axis, bit in BUTTERFLY:
        value = value + swap(value, axis, bit)
    return (write(summed, blocks), value[0])


def solution(mesh):
    split = Mesh(mesh.devices.reshape(SIZES), AXES)
    in_specs = (P(SAMPLES, "par"), P(SAMPLES))
    out_specs = (P(("zh", "x", "core", "par"), None, "zl"), P("par"))
    return jax.shard_map(body, mesh=split, in_specs=in_specs, out_specs=out_specs, check_vma=False)
```

```python
import jax
import jax.numpy as jnp
from jax import lax
from jax.experimental import pallas as pl
from jax.experimental.pallas import tpu as pltpu
from jax.sharding import Mesh, PartitionSpec as P

AXES = ("zl", "zh", "x", "core", "par")
SIZES = (4, 2, 4, 2, 8)
SAMPLES = AXES[:4]
LANES = 128
ORDER = (0, 1, 3, 2)
HOPS = (0, 1, 3, 2)
BUTTERFLY = (("core", 1), ("x", 1), ("x", 2), ("zh", 1), ("zl", 1), ("zl", 2))
VMEM = pltpu.CompilerParams(vmem_limit_bytes=24 * 1024 * 1024)


def shift(value, axis, by):
    count = lax.axis_size(axis)
    return lax.ppermute(value, axis, [(i, (i + by) % count) for i in range(count)])


def swap(value, axis, bit):
    return lax.ppermute(value, axis, [(i, i ^ bit) for i in range(lax.axis_size(axis))])


def halves(value):
    high = value.astype(jnp.bfloat16)
    low = (value - high.astype(jnp.float32)).astype(jnp.bfloat16)
    return high, low


def term_kernel(data_ref, vector_ref, term_ref):
    term_ref[...] = lax.dot_general(
        vector_ref[...],
        data_ref[...],
        (((1,), (0,)), ((), ())),
        precision=lax.Precision.HIGHEST,
        preferred_element_type=jnp.float32,
    )


def term(data, vector):
    local, params = data.shape
    return pl.pallas_call(
        term_kernel,
        out_shape=jax.ShapeDtypeStruct((1, params), jnp.float32),
        compiler_params=VMEM,
        cost_estimate=pl.CostEstimate(
            flops=12 * data.size, bytes_accessed=4 * data.size, transcendentals=0
        ),
    )(data, vector.reshape(1, local))


def left_kernel(left_ref, high_ref, low_ref, rows):
    blocks, local, params = left_ref.shape
    for g in range(params // LANES):
        lanes = pl.ds(g * LANES, LANES)
        for a in range(blocks):
            rows[g, pl.ds(ORDER[a], local, stride=blocks), :] = left_ref[a, :, lanes]
        high_ref[:, lanes], low_ref[:, lanes] = halves(rows[g])


def left_halves(left):
    blocks, local, params = left.shape
    shape = (blocks * local, params)
    return pl.pallas_call(
        left_kernel,
        out_shape=[jax.ShapeDtypeStruct(shape, jnp.bfloat16)] * 2,
        scratch_shapes=[pltpu.VMEM((params // LANES, blocks * local, LANES), jnp.float32)],
        compiler_params=VMEM,
        cost_estimate=pl.CostEstimate(
            flops=4 * left.size, bytes_accessed=8 * left.size, transcendentals=0
        ),
    )(left)


def multiply(high_ref, low_ref, mine_ref, other_ref, n, right):
    local = mine_ref.shape[1]
    core = lax.axis_index("core")
    right[pl.ds(pl.multiple_of(core * local, local), local), :] = mine_ref[n]
    right[pl.ds(pl.multiple_of((1 - core) * local, local), local), :] = other_ref[n]
    high, low = halves(right[...])

    def dot(a, b):
        return lax.dot_general(
            a, b, (((1,), (1,)), ((), ())), preferred_element_type=jnp.float32
        )

    return dot(high_ref[...], low) + dot(low_ref[...], high) + dot(high_ref[...], high)


def near_kernel(high_ref, low_ref, mine_ref, other_ref, out_ref, right):
    for n in range(out_ref.shape[0]):
        out_ref[n] = multiply(high_ref, low_ref, mine_ref, other_ref, n, right.at[n % 2])


def far_kernel(near_value, high_ref, low_ref, mine_ref, other_ref, total_hbm, far_value, right, sent):
    count, _, width = far_value.shape
    x, zh = lax.axis_index("x"), lax.axis_index("zh")

    def send(value, half, n):
        source = lax.rem(x + (count - HOPS[n % count]), count)
        first = pl.multiple_of((half * count + source) * width, width)
        return pltpu.make_async_copy(
            value.at[n % count], total_hbm.at[:, pl.ds(first, width)], sent.at[n]
        )

    copies = [send(near_value, zh, n) for n in range(count)]
    for copy in copies:
        copy.start()
    for n in range(count):
        far_value[n] = multiply(high_ref, low_ref, mine_ref, other_ref, n, right.at[n % 2])
        copies.append(send(far_value, 1 - zh, count + n))
        copies[-1].start()
    for copy in copies:
        copy.wait()


def product(left, near, near_other, far, far_other):
    rows, params = left[0].shape
    count, local, _ = near.shape
    width = 2 * local
    whole = pl.BlockSpec(memory_space=pltpu.VMEM)
    value = (count, rows, width)
    right = pltpu.VMEM((2, width, params), jnp.float32)
    cost = pl.CostEstimate(
        flops=6 * rows * count * width * params,
        bytes_accessed=4 * count * width * (params + rows),
        transcendentals=0,
    )
    near_value = pl.pallas_call(
        near_kernel,
        in_specs=[whole] * 4,
        out_specs=whole,
        out_shape=jax.ShapeDtypeStruct(value, jnp.float32),
        scratch_shapes=[right],
        compiler_params=VMEM,
        cost_estimate=cost,
    )(*left, near, near_other)
    return pl.pallas_call(
        far_kernel,
        in_specs=[whole] * 5,
        out_specs=pl.BlockSpec(memory_space=pltpu.HBM),
        out_shape=pltpu.HBM((rows, 2 * count * width), jnp.float32),
        scratch_shapes=[pltpu.VMEM(value, jnp.float32), right, pltpu.SemaphoreType.DMA((2 * count,))],
        compiler_params=VMEM,
        cost_estimate=cost,
    )(near_value, *left, far, far_other)


def body(log_derivs, sample_vector):
    left = lax.all_gather(log_derivs, "zl", axis_index_groups=[list(ORDER)])
    blocks = left.shape[0]

    far = swap(log_derivs, "zh", 1)
    near = jnp.stack([log_derivs] + [shift(log_derivs, "x", by) for by in HOPS[1:]])
    near_other = swap(near, "core", 1)
    far = jnp.stack([far] + [shift(far, "x", by) for by in HOPS[1:]])
    far, left = lax.optimization_barrier((far, left))
    far_other = swap(far, "core", 1)

    total = product(left_halves(left), near, near_other, far, far_other)
    total, log_derivs, sample_vector = lax.optimization_barrier((total, log_derivs, sample_vector))
    summed = lax.psum_scatter(total, "par", scatter_dimension=0, tiled=True)
    value = term(log_derivs, sample_vector)
    for axis, bit in BUTTERFLY:
        value = value + swap(value, axis, bit)
    return (summed.reshape(-1, blocks, summed.shape[1]), value[0])


def solution(mesh):
    split = Mesh(mesh.devices.reshape(SIZES), AXES)
    in_specs = (P(SAMPLES, "par"), P(SAMPLES))
    out_specs = (P(("zh", "x", "core", "par"), None, "zl"), P("par"))
    return jax.shard_map(body, mesh=split, in_specs=in_specs, out_specs=out_specs, check_vma=False)
```

```python
import jax
import jax.numpy as jnp
from jax import lax
from jax.experimental import pallas as pl
from jax.experimental.pallas import tpu as pltpu
from jax.sharding import Mesh, PartitionSpec as P

AXES = ("zl", "zh", "x", "core", "par")
SIZES = (4, 2, 4, 2, 8)
SAMPLES = AXES[:4]
LANES = 128
ORDER = (0, 1, 3, 2)
HOPS = (0, 2, 3, 1)
BUTTERFLY = (("core", 1), ("x", 1), ("x", 2), ("zh", 1), ("zl", 1), ("zl", 2))
VMEM = pltpu.CompilerParams(vmem_limit_bytes=24 * 1024 * 1024)


def shift(value, axis, by):
    count = lax.axis_size(axis)
    return lax.ppermute(value, axis, [(i, (i + by) % count) for i in range(count)])


def swap(value, axis, bit):
    return lax.ppermute(value, axis, [(i, i ^ bit) for i in range(lax.axis_size(axis))])


def halves(value):
    high = value.astype(jnp.bfloat16)
    low = (value - high.astype(jnp.float32)).astype(jnp.bfloat16)
    return high, low


def term_kernel(data_ref, vector_ref, term_ref):
    term_ref[...] = lax.dot_general(
        vector_ref[...],
        data_ref[...],
        (((1,), (0,)), ((), ())),
        precision=lax.Precision.HIGHEST,
        preferred_element_type=jnp.float32,
    )


def term(data, vector):
    local, params = data.shape
    return pl.pallas_call(
        term_kernel,
        out_shape=jax.ShapeDtypeStruct((1, params), jnp.float32),
        compiler_params=VMEM,
        cost_estimate=pl.CostEstimate(
            flops=12 * data.size, bytes_accessed=4 * data.size, transcendentals=0
        ),
    )(data, vector.reshape(1, local))


def left_kernel(left_ref, high_ref, low_ref, rows):
    blocks, local, params = left_ref.shape
    for g in range(params // LANES):
        lanes = pl.ds(g * LANES, LANES)
        for a in range(blocks):
            rows[g, pl.ds(ORDER[a], local, stride=blocks), :] = left_ref[a, :, lanes]
        high_ref[:, lanes], low_ref[:, lanes] = halves(rows[g])


def left_halves(left):
    blocks, local, params = left.shape
    shape = (blocks * local, params)
    return pl.pallas_call(
        left_kernel,
        out_shape=[jax.ShapeDtypeStruct(shape, jnp.bfloat16)] * 2,
        scratch_shapes=[pltpu.VMEM((params // LANES, blocks * local, LANES), jnp.float32)],
        compiler_params=VMEM,
        cost_estimate=pl.CostEstimate(
            flops=4 * left.size, bytes_accessed=8 * left.size, transcendentals=0
        ),
    )(left)


def multiply(high_ref, low_ref, mine_ref, other_ref, n, right):
    local = mine_ref.shape[1]
    core = lax.axis_index("core")
    right[pl.ds(pl.multiple_of(core * local, local), local), :] = mine_ref[n]
    right[pl.ds(pl.multiple_of((1 - core) * local, local), local), :] = other_ref[n]
    high, low = halves(right[...])

    def dot(a, b):
        return lax.dot_general(
            a, b, (((1,), (1,)), ((), ())), preferred_element_type=jnp.float32
        )

    return dot(high_ref[...], low) + dot(low_ref[...], high) + dot(high_ref[...], high)


def near_kernel(high_ref, low_ref, mine_ref, other_ref, out_ref, right):
    for n in range(out_ref.shape[0]):
        out_ref[n] = multiply(high_ref, low_ref, mine_ref, other_ref, n, right.at[n % 2])


def far_kernel(near_value, high_ref, low_ref, mine_ref, other_ref, total_hbm, far_value, right, sent):
    count, _, width = far_value.shape
    x, zh = lax.axis_index("x"), lax.axis_index("zh")

    def send(value, half, n):
        source = lax.rem(x + (count - HOPS[n % count]), count)
        first = pl.multiple_of((half * count + source) * width, width)
        return pltpu.make_async_copy(
            value.at[n % count], total_hbm.at[:, pl.ds(first, width)], sent.at[n]
        )

    copies = [send(near_value, zh, n) for n in range(count)]
    for copy in copies:
        copy.start()
    for n in range(count):
        far_value[n] = multiply(high_ref, low_ref, mine_ref, other_ref, n, right.at[n % 2])
        copies.append(send(far_value, 1 - zh, count + n))
        copies[-1].start()
    for copy in copies:
        copy.wait()


def product(left, near, near_other, far, far_other):
    rows, params = left[0].shape
    count, local, _ = near.shape
    width = 2 * local
    whole = pl.BlockSpec(memory_space=pltpu.VMEM)
    value = (count, rows, width)
    right = pltpu.VMEM((2, width, params), jnp.float32)
    cost = pl.CostEstimate(
        flops=6 * rows * count * width * params,
        bytes_accessed=4 * count * width * (params + rows),
        transcendentals=0,
    )
    near_value = pl.pallas_call(
        near_kernel,
        in_specs=[whole] * 4,
        out_specs=whole,
        out_shape=jax.ShapeDtypeStruct(value, jnp.float32),
        scratch_shapes=[right],
        compiler_params=VMEM,
        cost_estimate=cost,
    )(*left, near, near_other)
    return pl.pallas_call(
        far_kernel,
        in_specs=[whole] * 5,
        out_specs=pl.BlockSpec(memory_space=pltpu.HBM),
        out_shape=pltpu.HBM((rows, 2 * count * width), jnp.float32),
        scratch_shapes=[pltpu.VMEM(value, jnp.float32), right, pltpu.SemaphoreType.DMA((2 * count,))],
        compiler_params=VMEM,
        cost_estimate=cost,
    )(near_value, *left, far, far_other)


def body(log_derivs, sample_vector):
    left = lax.all_gather(log_derivs, "zl", axis_index_groups=[list(ORDER)])
    blocks = left.shape[0]

    far = swap(log_derivs, "zh", 1)
    near = jnp.stack([log_derivs] + [shift(log_derivs, "x", by) for by in HOPS[1:]])
    near_other = swap(near, "core", 1)
    far = jnp.stack([far] + [shift(far, "x", by) for by in HOPS[1:]])
    far, left = lax.optimization_barrier((far, left))
    far_other = swap(far, "core", 1)

    total = product(left_halves(left), near, near_other, far, far_other)
    total, log_derivs, sample_vector = lax.optimization_barrier((total, log_derivs, sample_vector))
    summed = lax.psum_scatter(total, "par", scatter_dimension=0, tiled=True)
    value = term(log_derivs, sample_vector)
    for axis, bit in BUTTERFLY:
        value = value + swap(value, axis, bit)
    return (summed.reshape(-1, blocks, summed.shape[1]), value[0])


def solution(mesh):
    split = Mesh(mesh.devices.reshape(SIZES), AXES)
    in_specs = (P(SAMPLES, "par"), P(SAMPLES))
    out_specs = (P(("zh", "x", "core", "par"), None, "zl"), P("par"))
    return jax.shard_map(body, mesh=split, in_specs=in_specs, out_specs=out_specs, check_vma=False)
```

```python
import jax
import jax.numpy as jnp
from jax import lax
from jax.experimental import pallas as pl
from jax.experimental.pallas import tpu as pltpu
from jax.sharding import Mesh, PartitionSpec as P

AXES = ("zl", "zh", "x", "core", "par")
SIZES = (4, 2, 4, 2, 8)
SAMPLES = AXES[:4]
LANES = 128
ORDER = (0, 1, 3, 2)
HOPS = (0, 1, 3, 2)
BUTTERFLY = (("core", 1), ("x", 1), ("x", 2), ("zh", 1), ("zl", 1), ("zl", 2))
VMEM = pltpu.CompilerParams(vmem_limit_bytes=24 * 1024 * 1024)


def shift(value, axis, by):
    count = lax.axis_size(axis)
    return lax.ppermute(value, axis, [(i, (i + by) % count) for i in range(count)])


def swap(value, axis, bit):
    return lax.ppermute(value, axis, [(i, i ^ bit) for i in range(lax.axis_size(axis))])


def halves(value):
    high = value.astype(jnp.bfloat16)
    low = (value - high.astype(jnp.float32)).astype(jnp.bfloat16)
    return high, low


def term_kernel(data_ref, vector_ref, term_ref):
    term_ref[...] = lax.dot_general(
        vector_ref[...],
        data_ref[...],
        (((1,), (0,)), ((), ())),
        precision=lax.Precision.HIGHEST,
        preferred_element_type=jnp.float32,
    )


def term(data, vector):
    local, params = data.shape
    return pl.pallas_call(
        term_kernel,
        out_shape=jax.ShapeDtypeStruct((1, params), jnp.float32),
        compiler_params=VMEM,
        cost_estimate=pl.CostEstimate(
            flops=12 * data.size, bytes_accessed=4 * data.size, transcendentals=0
        ),
    )(data, vector.reshape(1, local))


def left_kernel(left_ref, high_ref, low_ref, rows):
    blocks, local, params = left_ref.shape
    for g in range(params // LANES):
        lanes = pl.ds(g * LANES, LANES)
        for a in range(blocks):
            rows[g, pl.ds(ORDER[a], local, stride=blocks), :] = left_ref[a, :, lanes]
        high_ref[:, lanes], low_ref[:, lanes] = halves(rows[g])


def left_halves(left):
    blocks, local, params = left.shape
    shape = (blocks * local, params)
    return pl.pallas_call(
        left_kernel,
        out_shape=[jax.ShapeDtypeStruct(shape, jnp.bfloat16)] * 2,
        scratch_shapes=[pltpu.VMEM((params // LANES, blocks * local, LANES), jnp.float32)],
        compiler_params=VMEM,
        cost_estimate=pl.CostEstimate(
            flops=4 * left.size, bytes_accessed=8 * left.size, transcendentals=0
        ),
    )(left)


def multiply(high_ref, low_ref, mine_ref, other_ref, n, right):
    local = mine_ref.shape[1]
    core = lax.axis_index("core")
    right[pl.ds(pl.multiple_of(core * local, local), local), :] = mine_ref[n]
    right[pl.ds(pl.multiple_of((1 - core) * local, local), local), :] = other_ref[n]
    high, low = halves(right[...])

    def dot(a, b):
        return lax.dot_general(
            a, b, (((1,), (1,)), ((), ())), preferred_element_type=jnp.float32
        )

    return dot(high_ref[...], low) + dot(low_ref[...], high) + dot(high_ref[...], high)


def near_kernel(high_ref, low_ref, mine_ref, other_ref, out_ref, right):
    for n in range(out_ref.shape[0]):
        out_ref[n] = multiply(high_ref, low_ref, mine_ref, other_ref, n, right.at[n % 2])


def far_kernel(near_value, high_ref, low_ref, mine_ref, other_ref, total_hbm, far_value, right, sent):
    count, rows, width = far_value.shape
    x, zh = lax.axis_index("x"), lax.axis_index("zh")

    def send(value, half, n, part, parts):
        source = lax.rem(x + (count - HOPS[n % count]), count)
        first = pl.multiple_of((half * count + source) * width, width)
        some = pl.ds(part * (rows // parts), rows // parts)
        copies.append(
            pltpu.make_async_copy(
                value.at[n % count, some, :],
                total_hbm.at[some, pl.ds(first, width)],
                sent.at[len(copies)],
            )
        )
        copies[-1].start()

    copies = []
    for n in range(count):
        send(near_value, zh, n, 0, 1)
    for n in range(count):
        parts = 2 if n == count - 1 else 1
        for part in range(parts):
            some = pl.ds(part * (rows // parts), rows // parts)
            far_value[n, some, :] = multiply(
                high_ref.at[some], low_ref.at[some], mine_ref, other_ref, n, right.at[n % 2]
            )
            send(far_value, 1 - zh, count + n, part, parts)
    for copy in copies:
        copy.wait()


def product(left, near, near_other, far, far_other):
    rows, params = left[0].shape
    count, local, _ = near.shape
    width = 2 * local
    whole = pl.BlockSpec(memory_space=pltpu.VMEM)
    value = (count, rows, width)
    right = pltpu.VMEM((2, width, params), jnp.float32)
    cost = pl.CostEstimate(
        flops=6 * rows * count * width * params,
        bytes_accessed=4 * count * width * (params + rows),
        transcendentals=0,
    )
    near_value = pl.pallas_call(
        near_kernel,
        in_specs=[whole] * 4,
        out_specs=whole,
        out_shape=jax.ShapeDtypeStruct(value, jnp.float32),
        scratch_shapes=[right],
        compiler_params=VMEM,
        cost_estimate=cost,
    )(*left, near, near_other)
    return pl.pallas_call(
        far_kernel,
        in_specs=[whole] * 5,
        out_specs=pl.BlockSpec(memory_space=pltpu.HBM),
        out_shape=pltpu.HBM((rows, 2 * count * width), jnp.float32),
        scratch_shapes=[pltpu.VMEM(value, jnp.float32), right, pltpu.SemaphoreType.DMA((2 * count + 1,))],
        compiler_params=VMEM,
        cost_estimate=cost,
    )(near_value, *left, far, far_other)


def body(log_derivs, sample_vector):
    left = lax.all_gather(log_derivs, "zl", axis_index_groups=[list(ORDER)])
    blocks = left.shape[0]

    far = swap(log_derivs, "zh", 1)
    near = jnp.stack([log_derivs] + [shift(log_derivs, "x", by) for by in HOPS[1:]])
    near_other = swap(near, "core", 1)
    far = jnp.stack([far] + [shift(far, "x", by) for by in HOPS[1:]])
    far, left = lax.optimization_barrier((far, left))
    far_other = swap(far, "core", 1)

    total = product(left_halves(left), near, near_other, far, far_other)
    total, log_derivs, sample_vector = lax.optimization_barrier((total, log_derivs, sample_vector))
    summed = lax.psum_scatter(total, "par", scatter_dimension=0, tiled=True)
    value = term(log_derivs, sample_vector)
    for axis, bit in BUTTERFLY:
        value = value + swap(value, axis, bit)
    return (summed.reshape(-1, blocks, summed.shape[1]), value[0])


def solution(mesh):
    split = Mesh(mesh.devices.reshape(SIZES), AXES)
    in_specs = (P(SAMPLES, "par"), P(SAMPLES))
    out_specs = (P(("zh", "x", "core", "par"), None, "zl"), P("par"))
    return jax.shard_map(body, mesh=split, in_specs=in_specs, out_specs=out_specs, check_vma=False)
```

```python
import jax
import jax.numpy as jnp
from jax import lax
from jax.experimental import pallas as pl
from jax.experimental.pallas import tpu as pltpu
from jax.sharding import Mesh, PartitionSpec as P

AXES = ("zl", "zh", "x", "core", "par")
SIZES = (4, 2, 4, 2, 8)
SAMPLES = AXES[:4]
LANES = 128
ORDER = (0, 1, 3, 2)
HOPS = (0, 1, 3, 2)
BUTTERFLY = (("core", 1), ("x", 1), ("x", 2), ("zh", 1), ("zl", 1), ("zl", 2))
VMEM = pltpu.CompilerParams(vmem_limit_bytes=24 * 1024 * 1024)


def shift(value, axis, by):
    count = lax.axis_size(axis)
    return lax.ppermute(value, axis, [(i, (i + by) % count) for i in range(count)])


def swap(value, axis, bit):
    return lax.ppermute(value, axis, [(i, i ^ bit) for i in range(lax.axis_size(axis))])


def halves(value):
    high = value.astype(jnp.bfloat16)
    low = (value - high.astype(jnp.float32)).astype(jnp.bfloat16)
    return high, low


def term_kernel(data_ref, vector_ref, term_ref):
    term_ref[...] = lax.dot_general(
        vector_ref[...],
        data_ref[...],
        (((1,), (0,)), ((), ())),
        precision=lax.Precision.HIGHEST,
        preferred_element_type=jnp.float32,
    )


def term(data, vector):
    local, params = data.shape
    return pl.pallas_call(
        term_kernel,
        out_shape=jax.ShapeDtypeStruct((1, params), jnp.float32),
        compiler_params=VMEM,
        cost_estimate=pl.CostEstimate(
            flops=12 * data.size, bytes_accessed=4 * data.size, transcendentals=0
        ),
    )(data, vector.reshape(1, local))


def left_kernel(left_ref, high_ref, low_ref, rows):
    blocks, local, params = left_ref.shape
    for g in range(params // LANES):
        lanes = pl.ds(g * LANES, LANES)
        for a in range(blocks):
            rows[g, pl.ds(ORDER[a], local, stride=blocks), :] = left_ref[a, :, lanes]
        high_ref[:, lanes], low_ref[:, lanes] = halves(rows[g])


def left_halves(left):
    blocks, local, params = left.shape
    shape = (blocks * local, params)
    return pl.pallas_call(
        left_kernel,
        out_shape=[jax.ShapeDtypeStruct(shape, jnp.bfloat16)] * 2,
        scratch_shapes=[pltpu.VMEM((params // LANES, blocks * local, LANES), jnp.float32)],
        compiler_params=VMEM,
        cost_estimate=pl.CostEstimate(
            flops=4 * left.size, bytes_accessed=8 * left.size, transcendentals=0
        ),
    )(left)


def multiply(high_ref, low_ref, mine_ref, other_ref, n, right):
    local = mine_ref.shape[1]
    core = lax.axis_index("core")
    right[pl.ds(pl.multiple_of(core * local, local), local), :] = mine_ref[n]
    right[pl.ds(pl.multiple_of((1 - core) * local, local), local), :] = other_ref[n]
    high, low = halves(right[...])

    def dot(a, b):
        return lax.dot_general(
            a, b, (((1,), (1,)), ((), ())), preferred_element_type=jnp.float32
        )

    return dot(high_ref[...], low) + dot(low_ref[...], high) + dot(high_ref[...], high)


def near_kernel(high_ref, low_ref, mine_ref, other_ref, out_ref, right):
    for n in range(out_ref.shape[0]):
        out_ref[n] = multiply(high_ref, low_ref, mine_ref, other_ref, n, right.at[n % 2])


def far_kernel(near_value, high_ref, low_ref, mine_ref, other_ref, total_hbm, far_value, right, sent):
    count, _, width = far_value.shape
    x, zh = lax.axis_index("x"), lax.axis_index("zh")

    def send(value, half, n):
        source = lax.rem(x + (count - HOPS[n % count]), count)
        first = pl.multiple_of((half * count + source) * width, width)
        return pltpu.make_async_copy(
            value.at[n % count], total_hbm.at[:, pl.ds(first, width)], sent.at[n]
        )

    copies = [send(near_value, zh, n) for n in range(count)]
    for copy in copies:
        copy.start()
    for n in range(count):
        far_value[n] = multiply(high_ref, low_ref, mine_ref, other_ref, n, right.at[n % 2])
        copies.append(send(far_value, 1 - zh, count + n))
        copies[-1].start()
    for copy in copies:
        copy.wait()


def product(left, near, near_other, far, far_other):
    rows, params = left[0].shape
    count, local, _ = near.shape
    width = 2 * local
    whole = pl.BlockSpec(memory_space=pltpu.VMEM)
    value = (count, rows, width)
    right = pltpu.VMEM((2, width, params), jnp.float32)
    cost = pl.CostEstimate(
        flops=6 * rows * count * width * params,
        bytes_accessed=4 * count * width * (params + rows),
        transcendentals=0,
    )
    near_value = pl.pallas_call(
        near_kernel,
        in_specs=[whole] * 4,
        out_specs=whole,
        out_shape=jax.ShapeDtypeStruct(value, jnp.float32),
        scratch_shapes=[right],
        compiler_params=VMEM,
        cost_estimate=cost,
    )(*left, near, near_other)
    return pl.pallas_call(
        far_kernel,
        in_specs=[whole] * 5,
        out_specs=pl.BlockSpec(memory_space=pltpu.HBM),
        out_shape=pltpu.HBM((rows, 2 * count * width), jnp.float32),
        scratch_shapes=[pltpu.VMEM(value, jnp.float32), right, pltpu.SemaphoreType.DMA((2 * count,))],
        compiler_params=VMEM,
        cost_estimate=cost,
    )(near_value, *left, far, far_other)


def body(log_derivs, sample_vector):
    left = lax.all_gather(log_derivs, "zl", axis_index_groups=[list(ORDER)])
    blocks = left.shape[0]

    far = swap(log_derivs, "zh", 1)
    near = jnp.stack([log_derivs] + [shift(log_derivs, "x", by) for by in HOPS[1:]])
    near_other = swap(near, "core", 1)
    far = jnp.stack([far] + [shift(far, "x", by) for by in HOPS[1:]])
    left = left_halves(left)
    far, left = lax.optimization_barrier((far, left))
    far_other = swap(far, "core", 1)

    total = product(left, near, near_other, far, far_other)
    total, log_derivs, sample_vector = lax.optimization_barrier((total, log_derivs, sample_vector))
    summed = lax.psum_scatter(total, "par", scatter_dimension=0, tiled=True)
    value = term(log_derivs, sample_vector)
    for axis, bit in BUTTERFLY:
        value = value + swap(value, axis, bit)
    return (summed.reshape(-1, blocks, summed.shape[1]), value[0])


def solution(mesh):
    split = Mesh(mesh.devices.reshape(SIZES), AXES)
    in_specs = (P(SAMPLES, "par"), P(SAMPLES))
    out_specs = (P(("zh", "x", "core", "par"), None, "zl"), P("par"))
    return jax.shard_map(body, mesh=split, in_specs=in_specs, out_specs=out_specs, check_vma=False)
```
